32 devices in a mesh: dp: 2 (over x), expert: 4 (over z), tensor: 4 (over y, core).
Axes of the slice: x: 2, y: 2, z: 4, core: 2. Of those that a mesh axis runs over, the one named last changes fastest.
Arguments:
- tokens: bfloat16 [1024, 3584], P(('dp', 'expert'), 'tensor'), may hold values from -6 to 6
- cotangent: bfloat16 [1024, 3584], P(('dp', 'expert'), 'tensor'), may hold values from -6 to 6
- routes: int32 [1024, 2], P(('dp', 'expert')), may hold values from 0 to 3, all different within a row; in each aligned block of 128 rows (0 to 127, 128 to 255, ...) at most 80 rows name the same one
- route_weights: float32 [1024, 2], P(('dp', 'expert')), may hold values from 0.2 to 1
- gate_values: bfloat16 [4, 1792, 2560], P('expert', None, 'tensor'), may hold values from -0.125 to 0.125
- up_values: bfloat16 [4, 1792, 2560], P('expert', None, 'tensor'), may hold values from -0.125 to 0.125
- down_values: bfloat16 [4, 1280, 3584], P('expert', 'tensor'), may hold values from -0.15625 to 0.15625
- gate_words: int32 [4, 224, 2560], P('expert', None, 'tensor'), may hold values from 0 to 1295
- up_words: int32 [4, 224, 2560], P('expert', None, 'tensor'), may hold values from 0 to 1295
- down_words: int32 [4, 160, 3584], P('expert', 'tensor'), may hold values from 0 to 1295
- res_gate: bfloat16 [3584, 3072], P(None, ('dp', 'tensor')), may hold values from -0.09375 to 0.09375
- res_up: bfloat16 [3584, 3072], P(None, ('dp', 'tensor')), may hold values from -0.09375 to 0.09375
- res_down: bfloat16 [3584, 3072], P(None, ('dp', 'tensor')), may hold values from -0.109375 to 0.109375
Outputs:
- tokens_grad: bfloat16 [1024, 3584], P(('dp', 'expert'), 'tensor')
- gate_values_grad: bfloat16 [4, 1792, 2560], P('expert', 'dp', 'tensor')
- up_values_grad: bfloat16 [4, 1792, 2560], P('expert', 'dp', 'tensor')
- down_values_grad: bfloat16 [4, 1280, 3584], P('expert', 'tensor', 'dp')
- res_gate_grad: bfloat16 [3584, 3072], P('expert', ('dp', 'tensor'))
- res_up_grad: bfloat16 [3584, 3072], P('expert', ('dp', 'tensor'))
- res_down_grad: bfloat16 [3584, 3072], P('expert', ('dp', 'tensor'))
The draws below stay inside these ranges and needn't reach their ends.
Inputs may be any that keep to these rules, and one draw needn't show every extreme that they name: `routes`: each row names two different experts. Within the 128 rows of one token group no expert is named more than 80 times, a bound that some block reaches. `gate_words`: each entry is a word of four base-6 digits; digit k of entry [e, j, c] names the kept positions of the group of rows 16 * j + 4 * k to 16 * j + 4 * k + 3 in column c. `up_words`: laid out as gate_words. `down_words`: digit k of entry [e, j, c] names the kept positions of the group of hidden rows 16 * j + 4 * k to 16 * j + 4 * k + 3 in column c.
All inputs are finite; a program needn't handle non-finite values.
Results may differ from the reference program's by a relative error of at most 0.0095.
Values may be sent and summed in bfloat16 or wider, within the bound.
A program may use at most 256 MiB of HBM per device.

```python
import math
import jax
import jax.numpy as jnp
import numpy as np
from jax import lax

D = 3584
H = 2560
F = 3072
TOK_DEV = 128
EXPERTS = 4
GROUPS = 8
TOKENS = 1024
CAP = 80
N_DP = 2
N_EXPERT = 4


def touch_ends(drawn, own_key, least, largest):
    index_at = [jax.random.randint(jax.random.fold_in(own_key, axis), (), 0, length) for axis, length in enumerate(drawn.shape)]
    main_axis = drawn.shape.index(max(drawn.shape))
    neighbour = index_at[:main_axis] + [(index_at[main_axis] + 1) % drawn.shape[main_axis]] + index_at[main_axis + 1:]
    return drawn.at[tuple(index_at)].set(least).at[tuple(neighbour)].set(largest)


def raised(result, own_key, source, target, shards_of, factor):
    def block_of(dim):
        return (jnp.arange(result.shape[dim]) // (result.shape[dim] // shards_of)).reshape((-1,) + (1,) * (result.ndim - 1 - dim))

    one_side = jax.random.permutation(own_key, shards_of)[block_of(target)]
    far = (block_of(target) + shards_of // 2) % shards_of
    return jnp.where((block_of(source) == one_side) | (block_of(source) == far), factor * result, result)


def block_levels(stream_key, shape, shards, low, high):
    level, own = 1.0, jax.random.fold_in(stream_key, 6)
    for dim, blocks in shards:
        draws = jnp.exp(jax.random.uniform(jax.random.fold_in(own, dim), (blocks,), jnp.float32, low / len(shards), high / len(shards)))
        level = level * jnp.repeat(draws, shape[dim] // blocks).reshape([-1 if axis == dim else 1 for axis in range(len(shape))])
    return level


def assign_block(stream_key, own, number, rows, amount, top, bound, slope):
    order = jax.random.permutation(stream_key, amount)
    heavy_load, ordinary = shares(amount, rows * top, bound, slope, True), shares(amount, rows * top, bound, slope, False)
    places = jnp.arange(amount)

    def named(sizes, offset_by):
        used = int((sizes > 0).sum())
        fixed = max(1, used // 4)
        shifted = fixed + (places - fixed + offset_by * (used - fixed)) % max(1, amount - fixed)
        return jnp.zeros((amount,), jnp.int32).at[order[jnp.where(places < fixed, places, shifted)]].set(jnp.asarray(sizes, jnp.int32))

    sizes = jnp.where(number % 4 == 0, named(heavy_load, number // 4), named(ordinary, number - number // 4 - 1))
    mixed = jax.random.permutation(jax.random.fold_in(own, 3), amount)
    source_of, receiver = mixed[0:amount // 2 * 2:2], mixed[1:amount // 2 * 2:2]
    room = jnp.minimum(sizes[source_of] - 1, bound - sizes[receiver]) // 2
    room = jnp.where((source_of == order[0]) | (receiver == order[0]) | (sizes[receiver] == 0), 0, jnp.maximum(room, 0))
    shifted = jax.random.randint(jax.random.fold_in(own, 4), (amount // 2,), 0, 1 << 20) % (room + 1)
    sizes = sizes.at[source_of].add(-shifted).at[receiver].add(shifted)
    labels = jnp.searchsorted(jnp.cumsum(sizes), jnp.arange(rows * top), side="right").astype(jnp.int32)
    listing = labels.reshape(top, rows).T
    listing = listing[jax.random.permutation(jax.random.fold_in(own, 1), rows)]
    offset_by = jax.random.randint(jax.random.fold_in(own, 2), (rows, 1), 0, top)
    return jnp.take_along_axis(listing, (jnp.arange(top)[None, :] + offset_by) % top, axis=1)


def shares(number_of, total, limit, slope, full):
    loads = [(1 << 20) // math.isqrt(standing ** slope) + 1 for standing in range(1, number_of + 1)]
    largest = limit if full else min(limit, max(-(-total // number_of), total * loads[0] // sum(loads)))
    least = 1 if total - largest >= number_of - 1 else 0
    counts, surplus = [largest] + [least] * (number_of - 1), total - largest - least * (number_of - 1)
    while surplus > 0:
        free = [i for i in range(1, number_of) if counts[i] < largest] or [i for i in range(1, number_of) if counts[i] < limit]
        whole, budget = sum([loads[i] for i in free]), surplus
        for i in free:
            addition = min(limit - counts[i], max(1, budget * loads[i] // whole), surplus)
            counts[i] = counts[i] + addition
            surplus = surplus - addition
    return np.array(counts)


def scatter_about(own_key, shape, spread, most, shards=(), kind=jnp.bfloat16):
    level = block_levels(own_key, shape, shards, -0.22, 0.18) if shards else 1.0
    values = jax.random.normal(own_key, shape, jnp.float32) * spread * level
    return jnp.minimum(jnp.maximum(values, -most), most).astype(kind)


def noise_with(key, dims, scale, bound, split, heavy, kind=jnp.bfloat16):
    values = scale * jax.random.normal(key, dims, jnp.float32)
    if split:
        values = values * block_levels(key, dims, split, -0.22, 0.18)
    return jnp.clip(raised(values, jax.random.fold_in(key, 3), *heavy), -bound, bound).astype(kind)


def setup_inputs(seed: int = 0) -> dict:
    streams_of = jax.random.split(jax.random.key(seed), 14)
    tokens = noise_with(streams_of[0], (TOKENS, D), 1.0, 6.0, ((0, 8), (1, 4)), (0, 1, 8, 2.0))
    cotangent = scatter_about(streams_of[1], (TOKENS, D), 1.0, 6.0, ((0, 8), (1, 4)))
    routes_keys = jax.random.split(jax.random.fold_in(streams_of[2], 1), TOKENS // TOK_DEV)
    routes_turns = jax.random.permutation(jax.random.fold_in(streams_of[2], 3), TOKENS // TOK_DEV)
    routes = jax.vmap(lambda own, number: assign_block(jax.random.fold_in(streams_of[2], 2), own, number, TOK_DEV, EXPERTS, 2, CAP, 1))(routes_keys, routes_turns).reshape((TOKENS, 2))
    route_weights = jnp.clip(0.2 + 0.8 * jax.random.uniform(streams_of[3], (TOKENS, 2), jnp.float32) ** block_levels(streams_of[3], (TOKENS, 2), ((0, 8),), -0.2, 0.2), 0.2, 1.0)
    gate_values = scatter_about(streams_of[4], (EXPERTS, D // 2, H), (D // 2) ** -0.5, 0.125, ((0, 4), (2, 4)))
    up_values = scatter_about(streams_of[5], (EXPERTS, D // 2, H), (D // 2) ** -0.5, 0.125, ((0, 4), (2, 4)))
    down_values = scatter_about(streams_of[6], (EXPERTS, H // 2, D), (H // 2) ** -0.5, 0.15625, ((0, 4), (1, 4)))
    gate_words = touch_ends(jax.random.randint(streams_of[7], (EXPERTS, D // 16, H), 0, 1296), jax.random.fold_in(streams_of[7], 1), 0, 1295).astype(jnp.int32)
    up_words = touch_ends(jax.random.randint(streams_of[8], (EXPERTS, D // 16, H), 0, 1296), jax.random.fold_in(streams_of[8], 1), 0, 1295).astype(jnp.int32)
    down_words = touch_ends(jax.random.randint(streams_of[9], (EXPERTS, H // 16, D), 0, 1296), jax.random.fold_in(streams_of[9], 1), 0, 1295).astype(jnp.int32)
    res_gate = scatter_about(streams_of[10], (D, F), D ** -0.5, 0.09375, ((1, 8),))
    res_up = scatter_about(streams_of[11], (D, F), D ** -0.5, 0.09375, ((1, 8),))
    res_down = scatter_about(streams_of[12], (D, F), F ** -0.5, 0.109375, ((1, 8),))
    return {"tokens": tokens, "cotangent": cotangent, "routes": routes, "route_weights": route_weights, "gate_values": gate_values, "up_values": up_values, "down_values": down_values, "gate_words": gate_words, "up_words": up_words, "down_words": down_words, "res_gate": res_gate, "res_up": res_up, "res_down": res_down}


powers_six = (1, 6, 36, 216)


def kept_pair(word_rows):
    digits = jnp.stack([(word_rows // place_value) % 6 for place_value in powers_six], axis=1)
    pattern = digits.reshape((word_rows.shape[0] * 4,) + word_rows.shape[1:])
    past_three = (pattern >= 3).astype(jnp.int32)
    past_five = (pattern >= 5).astype(jnp.int32)
    return past_three + past_five, pattern + 1 - 2 * past_three - past_five


def expand_rows(values, word_rows):
    lead_pos, trail_pos = kept_pair(word_rows)
    paired = values.reshape((values.shape[0] // 2, 2) + values.shape[1:])
    places = jnp.arange(4, dtype=jnp.int32).reshape(1, 4, 1)
    nothing = jnp.zeros_like(paired[:, 0:1])
    dense = jnp.where(lead_pos[:, None] == places, paired[:, 0:1],
                      jnp.where(trail_pos[:, None] == places, paired[:, 1:2], nothing))
    return dense.reshape((values.shape[0] * 2,) + values.shape[1:])


def compress_rows(dense_grad, word_rows):
    lead_pos, trail_pos = kept_pair(word_rows)
    grouped = dense_grad.reshape((dense_grad.shape[0] // 4, 4) + dense_grad.shape[1:])
    places = jnp.arange(4, dtype=jnp.int32).reshape(1, 4, 1)
    nothing = jnp.zeros_like(grouped)
    lead_vals = jnp.sum(jnp.where(lead_pos[:, None] == places, grouped, nothing), axis=1)
    trail_vals = jnp.sum(jnp.where(trail_pos[:, None] == places, grouped, nothing), axis=1)
    return jnp.stack([lead_vals, trail_vals], axis=1).reshape((dense_grad.shape[0] // 2,) + dense_grad.shape[1:])


def slot_table(route_block, weight_block, experts, capacity):
    row_count = route_block.shape[0]
    flat_routes = route_block.reshape(-1).astype(jnp.int32)
    onehot = (flat_routes[:, None] == jnp.arange(experts, dtype=jnp.int32)[None, :]).astype(jnp.int32)
    before = jnp.cumsum(onehot, axis=0, dtype=jnp.int32) - onehot
    rank_in = jnp.sum(before * onehot, axis=1, dtype=jnp.int32)
    slot_index = (flat_routes * capacity + rank_in).astype(jnp.int32)
    owners = jnp.arange(2 * row_count, dtype=jnp.int32) // 2
    sources = jnp.full((experts * capacity,), row_count, jnp.int32).at[slot_index].set(owners)
    scales = jnp.zeros((experts * capacity,), jnp.float32).at[slot_index].set(weight_block.reshape(-1))
    return slot_index, sources, scales


def swiglu_back(row_block, cotangent_rows, w_gate, w_up, w_down):
    gate_pre = jnp.dot(row_block, w_gate, preferred_element_type=jnp.float32)
    up_pre = jnp.dot(row_block, w_up, preferred_element_type=jnp.float32)
    active = jax.nn.silu(gate_pre)
    hidden = (active * up_pre).astype(jnp.bfloat16)
    hid_grad = jnp.dot(cotangent_rows, w_down.T, preferred_element_type=jnp.float32)
    sigmoid_gate = jax.nn.sigmoid(gate_pre)
    gate_grad = (hid_grad * up_pre * sigmoid_gate * (1.0 + gate_pre * (1.0 - sigmoid_gate))).astype(jnp.bfloat16)
    up_grad = (hid_grad * active).astype(jnp.bfloat16)
    row_grad = (jnp.dot(gate_grad, w_gate.T, preferred_element_type=jnp.float32)
                + jnp.dot(up_grad, w_up.T, preferred_element_type=jnp.float32))
    gate_term = jnp.dot(row_block.T, gate_grad, preferred_element_type=jnp.float32)
    up_term = jnp.dot(row_block.T, up_grad, preferred_element_type=jnp.float32)
    down_term = jnp.dot(hidden.T, cotangent_rows, preferred_element_type=jnp.float32)
    return row_grad, gate_term, up_term, down_term


def settle(partial_term):
    return lax.optimization_barrier(partial_term.astype(jnp.bfloat16)).astype(jnp.float32)


def reference(tokens, cotangent, routes, route_weights, gate_values, up_values, down_values,
              gate_words, up_words, down_words, res_gate, res_up, res_down):
    tok_rows = tokens.reshape(GROUPS, TOK_DEV, D)
    cot_rows = cotangent.reshape(GROUPS, TOK_DEV, D)

    def table_of(route_block, weight_block):
        return slot_table(route_block, weight_block, EXPERTS, CAP)

    slot_index, sources, scales = jax.vmap(table_of)(routes.reshape(GROUPS, TOK_DEV, 2),
                                                     route_weights.reshape(GROUPS, TOK_DEV, 2))
    filler = jnp.zeros((GROUPS, 1, D), jnp.bfloat16)
    padded_tok = jnp.concatenate([tok_rows, filler], axis=1)
    padded_cot = jnp.concatenate([cot_rows, filler], axis=1)
    sent_tok = jnp.take_along_axis(padded_tok, sources[:, :, None], axis=1)
    sent_cot = (jnp.take_along_axis(padded_cot, sources[:, :, None], axis=1).astype(jnp.float32)
                * scales[:, :, None]).astype(jnp.bfloat16)
    arranged_tok = sent_tok.reshape(N_DP, N_EXPERT, EXPERTS, CAP, D).transpose(2, 0, 1, 3, 4)
    arranged_tok = arranged_tok.reshape(EXPERTS, N_DP, N_EXPERT * CAP, D)
    arranged_cot = sent_cot.reshape(N_DP, N_EXPERT, EXPERTS, CAP, D).transpose(2, 0, 1, 3, 4)
    arranged_cot = arranged_cot.reshape(EXPERTS, N_DP, N_EXPERT * CAP, D)

    def one_expert(operands):
        exp_tok, exp_cot, g_vals, u_vals, d_vals, g_words, u_words, d_words = operands
        gate_dense = expand_rows(g_vals, g_words)
        up_dense = expand_rows(u_vals, u_words)
        down_dense = expand_rows(d_vals, d_words)
        slot_grads = []
        gate_sum = jnp.zeros(g_vals.shape, jnp.float32)
        up_sum = jnp.zeros(u_vals.shape, jnp.float32)
        down_sum = jnp.zeros(d_vals.shape, jnp.float32)
        for member in range(N_DP):
            row_grad, gate_term, up_term, down_term = swiglu_back(exp_tok[member], exp_cot[member],
                                                                  gate_dense, up_dense, down_dense)
            slot_grads.append(row_grad)
            gate_sum = gate_sum + settle(compress_rows(gate_term, g_words))
            up_sum = up_sum + settle(compress_rows(up_term, u_words))
            down_sum = down_sum + settle(compress_rows(down_term, d_words))
        return (jnp.stack(slot_grads), gate_sum.astype(jnp.bfloat16), up_sum.astype(jnp.bfloat16),
                down_sum.astype(jnp.bfloat16))

    slot_back, gate_grads, up_grads, down_grads = lax.map(
        one_expert, (arranged_tok, arranged_cot, gate_values, up_values, down_values,
                     gate_words, up_words, down_words))
    returned = slot_back.reshape(EXPERTS, N_DP, N_EXPERT, CAP, D).transpose(1, 2, 0, 3, 4)
    returned = returned.reshape(GROUPS, EXPERTS * CAP, D)
    picked = jnp.take_along_axis(returned, slot_index[:, :, None], axis=1).reshape(GROUPS, TOK_DEV, 2, D)
    moe_grad = picked[:, :, 0] + picked[:, :, 1]

    pair_tok = tok_rows.reshape(N_DP, N_EXPERT, TOK_DEV, D).transpose(1, 0, 2, 3).reshape(
        N_EXPERT, N_DP * TOK_DEV, D)
    pair_cot = cot_rows.reshape(N_DP, N_EXPERT, TOK_DEV, D).transpose(1, 0, 2, 3).reshape(
        N_EXPERT, N_DP * TOK_DEV, D)

    def one_pair(carry, operands):
        row_block, cot_block = operands
        row_grad, gate_term, up_term, down_term = swiglu_back(row_block, cot_block, res_gate, res_up, res_down.T)
        updated = (carry[0] + settle(gate_term), carry[1] + settle(up_term), carry[2] + settle(down_term.T))
        return updated, row_grad

    empty = jnp.zeros((D, F), jnp.float32)
    res_sums, pair_grads = lax.scan(one_pair, (empty, empty, empty), (pair_tok, pair_cot))
    res_rows = pair_grads.reshape(N_EXPERT, N_DP, TOK_DEV, D).transpose(1, 0, 2, 3).reshape(GROUPS, TOK_DEV, D)
    tokens_grad = (res_rows + moe_grad).astype(jnp.bfloat16).reshape(TOKENS, D)
    return (tokens_grad, gate_grads, up_grads, down_grads, res_sums[0].astype(jnp.bfloat16),
            res_sums[1].astype(jnp.bfloat16), res_sums[2].astype(jnp.bfloat16))
```

```python
import functools

import jax
import jax.numpy as jnp
from jax import lax
from jax.experimental import pallas as pl
from jax.experimental.pallas import tpu as pltpu
from jax.sharding import PartitionSpec as P

VMEM_BYTES = 56 * 1024 * 1024


def call(body, **settings):
    return pl.pallas_call(
        body,
        compiler_params=pltpu.CompilerParams(vmem_limit_bytes=VMEM_BYTES),
        **settings,
    )


def mm(a, b, contract):
    return lax.dot_general(a, b, ((contract[:1], contract[1:]), ((), ())), preferred_element_type=jnp.float32)


def word_pieces(count):
    pieces, start = [], 0
    while start < count:
        size = 16 if count - start >= 16 else 8
        pieces.append((start, size))
        start += size
    return pieces


def kept_places(words):
    rest = words.astype(jnp.float32)
    digits = []
    for _ in range(3):
        above = jnp.floor((rest + 0.5) * (1.0 / 6.0))
        digits.append(rest - 6.0 * above)
        rest = above
    digits.append(rest)
    pattern = jnp.concatenate(digits, axis=0)
    three = jnp.where(pattern >= 3.0, 1.0, 0.0)
    five = jnp.where(pattern >= 5.0, 1.0, 0.0)
    return three + five, pattern + 1.0 - 2.0 * three - five


def value_order(size):
    n = 8 * size
    row = lax.broadcasted_iota(jnp.int32, (n, n), 0)
    col = lax.broadcasted_iota(jnp.int32, (n, n), 1)
    want = (col % 2) * (4 * size) + (col // 2 % 4) * size + col // 8
    return jnp.where(row == want, 1.0, 0.0).astype(jnp.bfloat16)


def dense_order(size):
    n = 16 * size
    row = lax.broadcasted_iota(jnp.int32, (n, n), 0)
    col = lax.broadcasted_iota(jnp.int32, (n, n), 1)
    want = (col % 4) * (4 * size) + (col // 4 % 4) * size + col // 16
    return jnp.where(row == want, 1.0, 0.0).astype(jnp.bfloat16)


def expand_body(values_ref, words_ref, dense_ref):
    for start, size in word_pieces(words_ref.shape[0]):
        lead, trail = kept_places(words_ref[start : start + size, :])
        both = mm(value_order(size), values_ref[8 * start : 8 * (start + size), :], (1, 0))
        half = 4 * size
        lead_vals, trail_vals = both[:half], both[half:]
        placed = jnp.concatenate(
            [
                jnp.where(lead == p, lead_vals, jnp.where(trail == p, trail_vals, 0.0))
                for p in (0.0, 1.0, 2.0, 3.0)
            ],
            axis=0,
        ).astype(jnp.bfloat16)
        dense_ref[16 * start : 16 * (start + size), :] = mm(dense_order(size), placed, (0, 0)).astype(
            jnp.bfloat16
        )


def expand(values, words, row_blocks, col_blocks):
    rows, cols = words.shape[0] // row_blocks, words.shape[1] // col_blocks
    at = lambda i: (i if row_blocks > 1 else 0, i if col_blocks > 1 else 0)
    return call(
        expand_body,
        grid=(row_blocks * col_blocks,),
        in_specs=[pl.BlockSpec((8 * rows, cols), at), pl.BlockSpec((rows, cols), at)],
        out_specs=pl.BlockSpec((16 * rows, cols), at),
        out_shape=jax.ShapeDtypeStruct((16 * words.shape[0], words.shape[1]), jnp.bfloat16),
        cost_estimate=pl.CostEstimate(flops=10**9 * 4, bytes_accessed=3 * 10**7, transcendentals=0),
    )(values, words)


def compress_into(dense, words_ref, out_ref):
    for start, size in word_pieces(words_ref.shape[0]):
        lead, trail = kept_places(words_ref[start : start + size, :])
        ordered = mm(dense_order(size), dense[16 * start : 16 * (start + size)], (1, 0))
        half = 4 * size
        lead_vals = jnp.zeros(lead.shape, jnp.float32)
        trail_vals = lead_vals
        for p in range(4):
            part = ordered[p * half : (p + 1) * half]
            lead_vals = jnp.where(lead == float(p), part, lead_vals)
            trail_vals = jnp.where(trail == float(p), part, trail_vals)
        both = jnp.concatenate([lead_vals, trail_vals], axis=0).astype(jnp.bfloat16)
        out_ref[8 * start : 8 * (start + size), :] = mm(value_order(size), both, (0, 0)).astype(
            jnp.bfloat16
        )


def swiglu_body(last, hidden_first, row_ref, cot_ref, gate_ref, up_ref, down_ref, *rest):
    hidden_ref, gate_grad_ref, up_grad_ref, gate_acc, up_acc, hid_acc = rest
    step = pl.program_id(0)

    @pl.when(step == 0)
    def _():
        gate_acc[...] = jnp.zeros_like(gate_acc)
        up_acc[...] = jnp.zeros_like(up_acc)
        hid_acc[...] = jnp.zeros_like(hid_acc)

    gate_acc[...] += mm(row_ref[0], gate_ref[...], (1, 0))
    up_acc[...] += mm(row_ref[0], up_ref[...], (1, 0))
    hid_acc[...] += mm(cot_ref[0], down_ref[...], (1, 1 if hidden_first else 0))

    @pl.when(step == last)
    def _():
        gate_pre, up_pre, hid_grad = gate_acc[...], up_acc[...], hid_acc[...]
        sig = jax.nn.sigmoid(gate_pre)
        active = gate_pre * sig
        hidden_ref[...] = (active * up_pre).astype(jnp.bfloat16)
        gate_grad_ref[...] = (hid_grad * up_pre * sig * (1.0 + gate_pre * (1.0 - sig))).astype(
            jnp.bfloat16
        )
        up_grad_ref[...] = (hid_grad * active).astype(jnp.bfloat16)


def swiglu_steps(both, w_gate, w_up, w_down, hidden_first):
    parts, rows, width = both.shape
    width //= 2
    hid = w_gate.shape[1]
    weight = pl.BlockSpec((width, hid), lambda i: (i, 0))
    down = pl.BlockSpec((hid, width), lambda i: (0, i)) if hidden_first else weight
    return call(
        functools.partial(swiglu_body, parts - 1, hidden_first),
        grid=(parts,),
        in_specs=[
            pl.BlockSpec((1, rows, width), lambda i: (i, 0, 0)),
            pl.BlockSpec((1, rows, width), lambda i: (i, 0, 1)),
            weight,
            weight,
            down,
        ],
        out_specs=[pl.BlockSpec((rows, hid), lambda i: (0, 0))] * 3,
        out_shape=[jax.ShapeDtypeStruct((rows, hid), jnp.bfloat16)] * 3,
        scratch_shapes=[pltpu.VMEM((rows, hid), jnp.float32)] * 3,
        cost_estimate=pl.CostEstimate(
            flops=6 * rows * hid * width * parts, bytes_accessed=2 * 10**7, transcendentals=rows * hid
        ),
    )(both, both, w_gate, w_up, w_down)


def back_body(gate_grad_ref, up_grad_ref, gate_ref, up_ref, out_ref):
    out_ref[0] = (
        mm(gate_grad_ref[...], gate_ref[...], (1, 1)) + mm(up_grad_ref[...], up_ref[...], (1, 1))
    ).astype(out_ref.dtype)


def back(gate_grad, up_grad, w_gate, w_up, parts):
    rows, hid = gate_grad.shape
    width = w_gate.shape[0] // parts
    whole = pl.BlockSpec((rows, hid), lambda i: (0, 0))
    weight = pl.BlockSpec((width, hid), lambda i: (i, 0))
    return call(
        back_body,
        grid=(parts,),
        in_specs=[whole, whole, weight, weight],
        out_specs=pl.BlockSpec((1, rows, width), lambda i: (i, 0, 0)),
        out_shape=jax.ShapeDtypeStruct((parts, rows, width), jnp.bfloat16),
        cost_estimate=pl.CostEstimate(
            flops=4 * rows * hid * width * parts, bytes_accessed=2 * 10**7, transcendentals=0
        ),
    )(gate_grad, up_grad, w_gate, w_up)


def gate_up_body(row_ref, gate_grad_ref, up_grad_ref, gate_words, up_words, gate_out, up_out):
    rows = row_ref[0]
    compress_into(mm(rows, gate_grad_ref[...], (0, 0)).astype(jnp.bfloat16), gate_words, gate_out)
    compress_into(mm(rows, up_grad_ref[...], (0, 0)).astype(jnp.bfloat16), up_words, up_out)


def gate_up_values(both, gate_grad, up_grad, gate_words, up_words):
    parts, rows, width = both.shape
    width //= 2
    hid = gate_grad.shape[1]
    grads = pl.BlockSpec((rows, hid), lambda i: (0, 0))
    words = pl.BlockSpec((width // 16, hid), lambda i: (i, 0))
    return call(
        gate_up_body,
        grid=(parts,),
        in_specs=[pl.BlockSpec((1, rows, width), lambda i: (i, 0, 0)), grads, grads, words, words],
        out_specs=[pl.BlockSpec((width // 2, hid), lambda i: (i, 0))] * 2,
        out_shape=[jax.ShapeDtypeStruct((parts * width // 2, hid), jnp.bfloat16)] * 2,
        cost_estimate=pl.CostEstimate(
            flops=8 * rows * hid * width * parts, bytes_accessed=2 * 10**7, transcendentals=0
        ),
    )(both, gate_grad, up_grad, gate_words, up_words)


def down_body(hidden_ref, cot_ref, words_ref, out_ref):
    compress_into(mm(hidden_ref[...], cot_ref[0], (0, 0)).astype(jnp.bfloat16), words_ref, out_ref)


def down_values_of(both, hidden, words):
    parts, rows, width = both.shape
    width //= 2
    hid = hidden.shape[1]
    return call(
        down_body,
        grid=(parts,),
        in_specs=[
            pl.BlockSpec((rows, hid), lambda i: (0, 0)),
            pl.BlockSpec((1, rows, width), lambda i: (i, 0, 1)),
            pl.BlockSpec((hid // 16, width), lambda i: (0, i)),
        ],
        out_specs=pl.BlockSpec((hid // 2, width), lambda i: (0, i)),
        out_shape=jax.ShapeDtypeStruct((hid // 2, parts * width), jnp.bfloat16),
        cost_estimate=pl.CostEstimate(
            flops=4 * rows * hid * width * parts, bytes_accessed=2 * 10**7, transcendentals=0
        ),
    )(hidden, both, words)


def weight_body(row_ref, cot_ref, gate_grad_ref, up_grad_ref, hidden_ref, *outs):
    rows, cots = row_ref[0], cot_ref[0]
    outs[0][...] = mm(rows, gate_grad_ref[...], (0, 0)).astype(jnp.bfloat16)
    outs[1][...] = mm(rows, up_grad_ref[...], (0, 0)).astype(jnp.bfloat16)
    outs[2][...] = mm(cots, hidden_ref[...], (0, 0)).astype(jnp.bfloat16)


def weight_grads(both, gate_grad, up_grad, hidden):
    parts, rows, width = both.shape
    width //= 2
    hid = hidden.shape[1]
    steps = pl.BlockSpec((rows, hid), lambda i: (0, 0))
    return call(
        weight_body,
        grid=(parts,),
        in_specs=[
            pl.BlockSpec((1, rows, width), lambda i: (i, 0, 0)),
            pl.BlockSpec((1, rows, width), lambda i: (i, 0, 1)),
            steps,
            steps,
            steps,
        ],
        out_specs=[pl.BlockSpec((width, hid), lambda i: (i, 0))] * 3,
        out_shape=[jax.ShapeDtypeStruct((parts * width, hid), jnp.bfloat16)] * 3,
        cost_estimate=pl.CostEstimate(
            flops=6 * rows * hid * width * parts, bytes_accessed=2 * 10**7, transcendentals=0
        ),
    )(both, both, gate_grad, up_grad, hidden)


def slot_masks(route_block, weight_block, experts, capacity):
    flat = route_block.reshape(-1)
    count = flat.shape[0]
    place = jnp.arange(count, dtype=jnp.int32)
    same = (flat[:, None] == flat[None, :]) & (place[None, :] < place[:, None])
    slot_index = flat * capacity + jnp.sum(same, axis=1, dtype=jnp.int32)
    slots = jnp.arange(experts * capacity, dtype=jnp.int32)
    first, second = slot_index.reshape(-1, 2)[:, 0], slot_index.reshape(-1, 2)[:, 1]
    hit_first = slots[:, None] == first[None, :]
    hit_second = slots[:, None] == second[None, :]
    taken = (hit_first | hit_second).astype(jnp.bfloat16)
    scales = jnp.sum(
        jnp.where(hit_first, weight_block[None, :, 0], 0.0)
        + jnp.where(hit_second, weight_block[None, :, 1], 0.0),
        axis=1,
    )
    return taken, scales


def shards(
    tokens,
    cotangent,
    routes,
    route_weights,
    gate_values,
    up_values,
    down_values,
    gate_words,
    up_words,
    down_words,
    res_gate,
    res_up,
    res_down,
):
    experts = lax.axis_size("expert")
    dp_count = lax.axis_size("dp")
    parts = lax.axis_size("tensor")
    tok_count, width = tokens.shape
    capacity = 5 * tok_count // (2 * experts)
    local = jnp.concatenate([tokens, cotangent], axis=1)
    pair_local = lax.all_gather(local, "dp", axis=0, tiled=True)
    pair_both = lax.all_gather(pair_local, "tensor", axis=0)
    taken, scales = slot_masks(routes, route_weights, experts, capacity)
    slot_local = mm(taken, local, (1, 0))
    slot_local = jnp.concatenate(
        [slot_local[:, :width], slot_local[:, width:] * scales[:, None]], axis=1
    ).astype(jnp.bfloat16)
    slot_local = lax.all_to_all(
        slot_local.reshape(experts, capacity, 2 * width), "expert", split_axis=0, concat_axis=0, tiled=True
    ).reshape(experts * capacity, 2 * width)
    slot_both = lax.all_gather(slot_local, "tensor", axis=0)

    gate_dense = expand(gate_values[0], gate_words[0], parts, 1)
    up_dense = expand(up_values[0], up_words[0], parts, 1)
    down_dense = expand(down_values[0], down_words[0], 1, parts)

    res_hidden, res_gate_step, res_up_step = swiglu_steps(pair_both, res_gate, res_up, res_down, False)
    res_back = back(res_gate_step, res_up_step, res_gate, res_up, parts)
    res_terms = weight_grads(pair_both, res_gate_step, res_up_step, res_hidden)

    hidden, gate_grad, up_grad = swiglu_steps(slot_both, gate_dense, up_dense, down_dense, True)
    slot_back = back(gate_grad, up_grad, gate_dense, up_dense, parts)
    gate_terms, up_terms = gate_up_values(slot_both, gate_grad, up_grad, gate_words[0], up_words[0])
    down_terms = down_values_of(slot_both, hidden, down_words[0])

    both_back = jnp.concatenate([slot_back, res_back], axis=1)
    both_share = lax.psum_scatter(both_back, "tensor", scatter_dimension=0, tiled=True)[0]
    slot_count = experts * capacity
    returned = lax.all_to_all(
        both_share[:slot_count].reshape(experts, capacity, width),
        "expert",
        split_axis=0,
        concat_axis=0,
        tiled=True,
    ).reshape(slot_count, width)
    res_share = lax.psum_scatter(both_share[slot_count:], "dp", scatter_dimension=0, tiled=True)
    combined = res_share.astype(jnp.float32) + mm(taken, returned, (0, 0))

    gate_share = lax.psum_scatter(gate_terms, "dp", scatter_dimension=0, tiled=True)
    up_share = lax.psum_scatter(up_terms, "dp", scatter_dimension=0, tiled=True)
    down_share = lax.psum_scatter(down_terms, "dp", scatter_dimension=1, tiled=True)
    res_sums = [lax.psum_scatter(term, "expert", scatter_dimension=0, tiled=True) for term in res_terms]
    return (
        combined.astype(jnp.bfloat16),
        gate_share[None],
        up_share[None],
        down_share[None],
        res_sums[0],
        res_sums[1],
        res_sums[2],
    )


def solution(mesh):
    in_specs = (
        P(("dp", "expert"), "tensor"),
        P(("dp", "expert"), "tensor"),
        P(("dp", "expert"), None),
        P(("dp", "expert"), None),
        P("expert", None, "tensor"),
        P("expert", None, "tensor"),
        P("expert", "tensor", None),
        P("expert", None, "tensor"),
        P("expert", None, "tensor"),
        P("expert", "tensor", None),
        P(None, ("dp", "tensor")),
        P(None, ("dp", "tensor")),
        P(None, ("dp", "tensor")),
    )
    out_specs = (
        P(("dp", "expert"), "tensor"),
        P("expert", "dp", "tensor"),
        P("expert", "dp", "tensor"),
        P("expert", "tensor", "dp"),
        P("expert", ("dp", "tensor")),
        P("expert", ("dp", "tensor")),
        P("expert", ("dp", "tensor")),
    )
    return jax.shard_map(shards, mesh=mesh, in_specs=in_specs, out_specs=out_specs, check_vma=False)
```

```python
import functools

import jax
import jax.numpy as jnp
from jax import lax
from jax.experimental import pallas as pl
from jax.experimental.pallas import tpu as pltpu
from jax.sharding import PartitionSpec as P

VMEM_BYTES = 56 * 1024 * 1024


def call(body, **settings):
    return pl.pallas_call(
        body,
        compiler_params=pltpu.CompilerParams(vmem_limit_bytes=VMEM_BYTES),
        **settings,
    )


def mm(a, b, contract):
    return lax.dot_general(a, b, ((contract[:1], contract[1:]), ((), ())), preferred_element_type=jnp.float32)


def word_pieces(count):
    pieces, start = [], 0
    while start < count:
        size = 16 if count - start >= 16 else 8
        pieces.append((start, size))
        start += size
    return pieces


def kept_places(words):
    rest = words.astype(jnp.float32)
    digits = []
    for _ in range(3):
        above = jnp.floor((rest + 0.5) * (1.0 / 6.0))
        digits.append(rest - 6.0 * above)
        rest = above
    digits.append(rest)
    pattern = jnp.concatenate(digits, axis=0)
    three = jnp.where(pattern >= 3.0, 1.0, 0.0)
    five = jnp.where(pattern >= 5.0, 1.0, 0.0)
    return three + five, pattern + 1.0 - 2.0 * three - five


def value_order(size):
    n = 8 * size
    row = lax.broadcasted_iota(jnp.int32, (n, n), 0)
    col = lax.broadcasted_iota(jnp.int32, (n, n), 1)
    want = (col % 2) * (4 * size) + (col // 2 % 4) * size + col // 8
    return jnp.where(row == want, 1.0, 0.0).astype(jnp.bfloat16)


def dense_order(size):
    n = 16 * size
    row = lax.broadcasted_iota(jnp.int32, (n, n), 0)
    col = lax.broadcasted_iota(jnp.int32, (n, n), 1)
    want = (col % 4) * (4 * size) + (col // 4 % 4) * size + col // 16
    return jnp.where(row == want, 1.0, 0.0).astype(jnp.bfloat16)


def expand_body(values_ref, words_ref, dense_ref):
    for start, size in word_pieces(words_ref.shape[0]):
        lead, trail = kept_places(words_ref[start : start + size, :])
        both = mm(value_order(size), values_ref[8 * start : 8 * (start + size), :], (1, 0))
        half = 4 * size
        lead_vals, trail_vals = both[:half], both[half:]
        placed = jnp.concatenate(
            [
                jnp.where(lead == p, lead_vals, jnp.where(trail == p, trail_vals, 0.0))
                for p in (0.0, 1.0, 2.0, 3.0)
            ],
            axis=0,
        ).astype(jnp.bfloat16)
        dense_ref[16 * start : 16 * (start + size), :] = mm(dense_order(size), placed, (0, 0)).astype(
            jnp.bfloat16
        )


def expand(values, words, row_blocks, col_blocks):
    rows, cols = words.shape[0] // row_blocks, words.shape[1] // col_blocks
    at = lambda i: (i if row_blocks > 1 else 0, i if col_blocks > 1 else 0)
    return call(
        expand_body,
        grid=(row_blocks * col_blocks,),
        in_specs=[pl.BlockSpec((8 * rows, cols), at), pl.BlockSpec((rows, cols), at)],
        out_specs=pl.BlockSpec((16 * rows, cols), at),
        out_shape=jax.ShapeDtypeStruct((16 * words.shape[0], words.shape[1]), jnp.bfloat16),
        cost_estimate=pl.CostEstimate(flops=10**9 * 4, bytes_accessed=3 * 10**7, transcendentals=0),
    )(values, words)


def compress_into(dense, words_ref, out_ref):
    for start, size in word_pieces(words_ref.shape[0]):
        lead, trail = kept_places(words_ref[start : start + size, :])
        ordered = mm(dense_order(size), dense[16 * start : 16 * (start + size)], (1, 0))
        half = 4 * size
        lead_vals = jnp.zeros(lead.shape, jnp.float32)
        trail_vals = lead_vals
        for p in range(4):
            part = ordered[p * half : (p + 1) * half]
            lead_vals = jnp.where(lead == float(p), part, lead_vals)
            trail_vals = jnp.where(trail == float(p), part, trail_vals)
        both = jnp.concatenate([lead_vals, trail_vals], axis=0).astype(jnp.bfloat16)
        out_ref[8 * start : 8 * (start + size), :] = mm(value_order(size), both, (0, 0)).astype(
            jnp.bfloat16
        )


def swiglu_body(last, hidden_first, row_ref, cot_ref, gate_ref, up_ref, down_ref, *rest):
    hidden_ref, gate_grad_ref, up_grad_ref, gate_acc, up_acc, hid_acc = rest
    step = pl.program_id(0)

    @pl.when(step == 0)
    def _():
        gate_acc[...] = jnp.zeros_like(gate_acc)
        up_acc[...] = jnp.zeros_like(up_acc)
        hid_acc[...] = jnp.zeros_like(hid_acc)

    gate_acc[...] += mm(row_ref[0], gate_ref[...], (1, 0))
    up_acc[...] += mm(row_ref[0], up_ref[...], (1, 0))
    hid_acc[...] += mm(cot_ref[0], down_ref[...], (1, 1 if hidden_first else 0))

    @pl.when(step == last)
    def _():
        gate_pre, up_pre, hid_grad = gate_acc[...], up_acc[...], hid_acc[...]
        sig = jax.nn.sigmoid(gate_pre)
        active = gate_pre * sig
        hidden_ref[...] = (active * up_pre).astype(jnp.bfloat16)
        gate_grad_ref[...] = (hid_grad * up_pre * sig * (1.0 + gate_pre * (1.0 - sig))).astype(
            jnp.bfloat16
        )
        up_grad_ref[...] = (hid_grad * active).astype(jnp.bfloat16)


def swiglu_steps(both, w_gate, w_up, w_down, hidden_first):
    parts, rows, width = both.shape
    width //= 2
    hid = w_gate.shape[1]
    weight = pl.BlockSpec((width, hid), lambda i: (i, 0))
    down = pl.BlockSpec((hid, width), lambda i: (0, i)) if hidden_first else weight
    return call(
        functools.partial(swiglu_body, parts - 1, hidden_first),
        grid=(parts,),
        in_specs=[
            pl.BlockSpec((1, rows, width), lambda i: (i, 0, 0)),
            pl.BlockSpec((1, rows, width), lambda i: (i, 0, 1)),
            weight,
            weight,
            down,
        ],
        out_specs=[pl.BlockSpec((rows, hid), lambda i: (0, 0))] * 3,
        out_shape=[jax.ShapeDtypeStruct((rows, hid), jnp.bfloat16)] * 3,
        scratch_shapes=[pltpu.VMEM((rows, hid), jnp.float32)] * 3,
        cost_estimate=pl.CostEstimate(
            flops=6 * rows * hid * width * parts, bytes_accessed=2 * 10**7, transcendentals=rows * hid
        ),
    )(both, both, w_gate, w_up, w_down)


def back_body(gate_grad_ref, up_grad_ref, gate_ref, up_ref, out_ref):
    out_ref[0] = (
        mm(gate_grad_ref[...], gate_ref[...], (1, 1)) + mm(up_grad_ref[...], up_ref[...], (1, 1))
    ).astype(out_ref.dtype)


def back(gate_grad, up_grad, w_gate, w_up, parts):
    rows, hid = gate_grad.shape
    width = w_gate.shape[0] // parts
    whole = pl.BlockSpec((rows, hid), lambda i: (0, 0))
    weight = pl.BlockSpec((width, hid), lambda i: (i, 0))
    return call(
        back_body,
        grid=(parts,),
        in_specs=[whole, whole, weight, weight],
        out_specs=pl.BlockSpec((1, rows, width), lambda i: (i, 0, 0)),
        out_shape=jax.ShapeDtypeStruct((parts, rows, width), jnp.bfloat16),
        cost_estimate=pl.CostEstimate(
            flops=4 * rows * hid * width * parts, bytes_accessed=2 * 10**7, transcendentals=0
        ),
    )(gate_grad, up_grad, w_gate, w_up)


def gate_up_body(row_ref, gate_grad_ref, up_grad_ref, gate_words, up_words, gate_out, up_out):
    rows = row_ref[0]
    compress_into(mm(rows, gate_grad_ref[...], (0, 0)).astype(jnp.bfloat16), gate_words, gate_out)
    compress_into(mm(rows, up_grad_ref[...], (0, 0)).astype(jnp.bfloat16), up_words, up_out)


def gate_up_values(both, gate_grad, up_grad, gate_words, up_words):
    parts, rows, width = both.shape
    width //= 2
    hid = gate_grad.shape[1]
    grads = pl.BlockSpec((rows, hid), lambda i: (0, 0))
    words = pl.BlockSpec((width // 16, hid), lambda i: (i, 0))
    return call(
        gate_up_body,
        grid=(parts,),
        in_specs=[pl.BlockSpec((1, rows, width), lambda i: (i, 0, 0)), grads, grads, words, words],
        out_specs=[pl.BlockSpec((width // 2, hid), lambda i: (i, 0))] * 2,
        out_shape=[jax.ShapeDtypeStruct((parts * width // 2, hid), jnp.bfloat16)] * 2,
        cost_estimate=pl.CostEstimate(
            flops=8 * rows * hid * width * parts, bytes_accessed=2 * 10**7, transcendentals=0
        ),
    )(both, gate_grad, up_grad, gate_words, up_words)


def down_body(hidden_ref, cot_ref, words_ref, out_ref):
    compress_into(mm(hidden_ref[...], cot_ref[0], (0, 0)).astype(jnp.bfloat16), words_ref, out_ref)


def down_values_of(both, hidden, words):
    parts, rows, width = both.shape
    width //= 2
    hid = hidden.shape[1]
    return call(
        down_body,
        grid=(parts,),
        in_specs=[
            pl.BlockSpec((rows, hid), lambda i: (0, 0)),
            pl.BlockSpec((1, rows, width), lambda i: (i, 0, 1)),
            pl.BlockSpec((hid // 16, width), lambda i: (0, i)),
        ],
        out_specs=pl.BlockSpec((hid // 2, width), lambda i: (0, i)),
        out_shape=jax.ShapeDtypeStruct((hid // 2, parts * width), jnp.bfloat16),
        cost_estimate=pl.CostEstimate(
            flops=4 * rows * hid * width * parts, bytes_accessed=2 * 10**7, transcendentals=0
        ),
    )(hidden, both, words)


def weight_body(row_ref, cot_ref, steps_ref, *outs):
    hid = steps_ref.shape[1] // 3
    rows, cots = row_ref[0], cot_ref[0]
    outs[0][...] = mm(rows, steps_ref[:, :hid], (0, 0)).astype(jnp.bfloat16)
    outs[1][...] = mm(rows, steps_ref[:, hid : 2 * hid], (0, 0)).astype(jnp.bfloat16)
    outs[2][...] = mm(cots, steps_ref[:, 2 * hid :], (0, 0)).astype(jnp.bfloat16)


def weight_grads(both, steps):
    parts, rows, width = both.shape
    width //= 2
    hid = steps.shape[1] // 3
    cuts = 7 if width % 896 == 0 and parts == 1 else 1
    piece = width // cuts
    return call(
        weight_body,
        grid=(parts, cuts),
        in_specs=[
            pl.BlockSpec((1, rows, piece), lambda i, j: (i, 0, j)),
            pl.BlockSpec((1, rows, piece), lambda i, j: (i, 0, cuts + j)),
            pl.BlockSpec((rows, 3 * hid), lambda i, j: (0, 0)),
        ],
        out_specs=[pl.BlockSpec((piece, hid), lambda i, j: (i * cuts + j, 0))] * 3,
        out_shape=[jax.ShapeDtypeStruct((parts * width, hid), jnp.bfloat16)] * 3,
        cost_estimate=pl.CostEstimate(
            flops=6 * rows * hid * width * parts, bytes_accessed=2 * 10**7, transcendentals=0
        ),
    )(both, both, steps)


def slot_masks(route_block, weight_block, own, experts, capacity):
    flat = (route_block.reshape(-1) - own + experts) % experts
    count = flat.shape[0]
    place = jnp.arange(count, dtype=jnp.int32)
    same = (flat[:, None] == flat[None, :]) & (place[None, :] < place[:, None])
    slot_index = flat * capacity + jnp.sum(same, axis=1, dtype=jnp.int32)
    slots = jnp.arange(experts * capacity, dtype=jnp.int32)
    first, second = slot_index.reshape(-1, 2)[:, 0], slot_index.reshape(-1, 2)[:, 1]
    hit_first = slots[:, None] == first[None, :]
    hit_second = slots[:, None] == second[None, :]
    taken = (hit_first | hit_second).astype(jnp.bfloat16)
    scales = jnp.sum(
        jnp.where(hit_first, weight_block[None, :, 0], 0.0)
        + jnp.where(hit_second, weight_block[None, :, 1], 0.0),
        axis=1,
    )
    return taken, scales


def swapped(block, axis, distance):
    count = lax.axis_size(axis)
    return lax.ppermute(block, axis, [(i, i ^ distance) for i in range(count)])


def shifted(block, axis, distance):
    count = lax.axis_size(axis)
    return lax.ppermute(block, axis, [(i, (i + distance) % count) for i in range(count)])


def gather_parts(block):
    if lax.axis_size("tensor") != 4:
        return lax.all_gather(block, "tensor", axis=0)
    place = lax.axis_index("tensor")
    low_chip, low_core = place // 2 == 0, place % 2 == 0
    far = swapped(block, "tensor", 2)
    mine = jnp.stack([jnp.where(low_chip, block, far), jnp.where(low_chip, far, block)])
    near = swapped(mine, "tensor", 1)
    both = jnp.stack([jnp.where(low_core, mine, near), jnp.where(low_core, near, mine)], axis=1)
    return both.reshape((4,) + block.shape)


def added(a, b):
    return a.astype(jnp.float32) + b.astype(jnp.float32)


def scatter_parts(parts):
    if lax.axis_size("tensor") != 4:
        return lax.psum_scatter(parts, "tensor", scatter_dimension=0, tiled=True)[0].astype(jnp.float32)
    place = lax.axis_index("tensor")
    chip, core = place // 2, place % 2
    split = parts.reshape((2, 2) + parts.shape[1:])
    send = lax.dynamic_index_in_dim(split, 1 - core, 1, keepdims=False)
    keep = lax.dynamic_index_in_dim(split, core, 1, keepdims=False)
    summed = added(keep, swapped(send, "tensor", 1)).astype(jnp.bfloat16)
    send = lax.dynamic_index_in_dim(summed, 1 - chip, 0, keepdims=False)
    keep = lax.dynamic_index_in_dim(summed, chip, 0, keepdims=False)
    return added(keep, swapped(send, "tensor", 2))


def scatter_batches(block, axis):
    if lax.axis_size("dp") != 2:
        return lax.psum_scatter(block, "dp", scatter_dimension=axis, tiled=True).astype(jnp.float32)
    own = lax.axis_index("dp")
    size = block.shape[axis] // 2
    send = lax.dynamic_slice_in_dim(block, (1 - own) * size, size, axis)
    keep = lax.dynamic_slice_in_dim(block, own * size, size, axis)
    return added(keep, swapped(send, "dp", 1))


def shards(
    tokens,
    cotangent,
    routes,
    route_weights,
    gate_values,
    up_values,
    down_values,
    gate_words,
    up_words,
    down_words,
    res_gate,
    res_up,
    res_down,
):
    experts = lax.axis_size("expert")
    dp_count = lax.axis_size("dp")
    parts = lax.axis_size("tensor")
    tok_count, width = tokens.shape
    capacity = 5 * tok_count // (2 * experts)
    local = jnp.concatenate([tokens, cotangent], axis=1)
    taken, scales = slot_masks(routes, route_weights, lax.axis_index("expert"), experts, capacity)
    slot_local = mm(taken, local, (1, 0))
    slot_local = jnp.concatenate(
        [slot_local[:, :width], slot_local[:, width:] * scales[:, None]], axis=1
    ).astype(jnp.bfloat16)
    blocks = [slot_local[k * capacity : (k + 1) * capacity] for k in range(experts)]
    arrived = [blocks[0]] + [shifted(blocks[k], "expert", k) for k in range(1, experts)]
    slot_both = gather_parts(jnp.concatenate(arrived, axis=0))

    pair_both = lax.all_gather(local, ("tensor", "dp"), axis=0).reshape(
        parts, dp_count * tok_count, 2 * width
    )

    gate_dense = expand(gate_values[0], gate_words[0], parts, 1)
    up_dense = expand(up_values[0], up_words[0], parts, 1)
    down_dense = expand(down_values[0], down_words[0], 1, parts)

    res_hidden, res_gate_step, res_up_step = swiglu_steps(pair_both, res_gate, res_up, res_down, False)
    res_back = back(res_gate_step, res_up_step, res_gate, res_up, parts)

    hidden, gate_grad, up_grad = swiglu_steps(slot_both, gate_dense, up_dense, down_dense, True)
    slot_back = back(gate_grad, up_grad, gate_dense, up_dense, parts)
    gate_terms, up_terms = gate_up_values(slot_both, gate_grad, up_grad, gate_words[0], up_words[0])
    down_terms = down_values_of(slot_both, hidden, down_words[0])

    slot_share = scatter_parts(slot_back).astype(jnp.bfloat16)
    blocks = [slot_share[k * capacity : (k + 1) * capacity] for k in range(experts)]
    returned = [blocks[0]] + [shifted(blocks[k], "expert", -k) for k in range(1, experts)]
    res_share = scatter_batches(scatter_parts(res_back).astype(jnp.bfloat16), 0)
    combined = res_share + mm(taken, jnp.concatenate(returned, axis=0), (0, 0))

    gate_share = scatter_batches(gate_terms, 0)
    up_share = scatter_batches(up_terms, 0)
    down_share = scatter_batches(down_terms, 1)

    if parts == experts:
        turned = lax.ppermute(
            local,
            ("expert", "tensor"),
            [(e * parts + t, t * parts + e) for e in range(experts) for t in range(parts)],
        )
        all_rows = lax.all_gather(turned, ("tensor", "dp"), axis=0).reshape(1, -1, 2 * width)
        steps = jnp.concatenate([res_gate_step, res_up_step, res_hidden], axis=1)
        steps = lax.all_gather(steps, "expert", axis=0, tiled=True)
        res_sums = weight_grads(all_rows, steps)
    else:
        steps = jnp.concatenate([res_gate_step, res_up_step, res_hidden], axis=1)
        res_sums = [
            lax.psum_scatter(term, "expert", scatter_dimension=0, tiled=True)
            for term in weight_grads(pair_both, steps)
        ]
    return (
        combined.astype(jnp.bfloat16),
        gate_share.astype(jnp.bfloat16)[None],
        up_share.astype(jnp.bfloat16)[None],
        down_share.astype(jnp.bfloat16)[None],
        res_sums[0],
        res_sums[1],
        res_sums[2],
    )


def solution(mesh):
    in_specs = (
        P(("dp", "expert"), "tensor"),
        P(("dp", "expert"), "tensor"),
        P(("dp", "expert"), None),
        P(("dp", "expert"), None),
        P("expert", None, "tensor"),
        P("expert", None, "tensor"),
        P("expert", "tensor", None),
        P("expert", None, "tensor"),
        P("expert", None, "tensor"),
        P("expert", "tensor", None),
        P(None, ("dp", "tensor")),
        P(None, ("dp", "tensor")),
        P(None, ("dp", "tensor")),
    )
    out_specs = (
        P(("dp", "expert"), "tensor"),
        P("expert", "dp", "tensor"),
        P("expert", "dp", "tensor"),
        P("expert", "tensor", "dp"),
        P("expert", ("dp", "tensor")),
        P("expert", ("dp", "tensor")),
        P("expert", ("dp", "tensor")),
    )
    return jax.shard_map(shards, mesh=mesh, in_specs=in_specs, out_specs=out_specs, check_vma=False)
```

```python
import functools

import jax
import jax.numpy as jnp
from jax import lax
from jax.experimental import pallas as pl
from jax.experimental.pallas import tpu as pltpu
from jax.sharding import PartitionSpec as P

VMEM_BYTES = 56 * 1024 * 1024


def call(body, **settings):
    return pl.pallas_call(
        body,
        compiler_params=pltpu.CompilerParams(vmem_limit_bytes=VMEM_BYTES),
        **settings,
    )


def mm(a, b, contract):
    return lax.dot_general(a, b, ((contract[:1], contract[1:]), ((), ())), preferred_element_type=jnp.float32)


def word_pieces(count):
    pieces, start = [], 0
    while start < count:
        size = 16 if count - start >= 16 else 8
        pieces.append((start, size))
        start += size
    return pieces


def kept_places(words):
    rest = words.astype(jnp.float32)
    digits = []
    for _ in range(3):
        above = jnp.floor((rest + 0.5) * (1.0 / 6.0))
        digits.append(rest - 6.0 * above)
        rest = above
    digits.append(rest)
    pattern = jnp.concatenate(digits, axis=0)
    three = jnp.where(pattern >= 3.0, 1.0, 0.0)
    five = jnp.where(pattern >= 5.0, 1.0, 0.0)
    return three + five, pattern + 1.0 - 2.0 * three - five


def value_order(size):
    n = 8 * size
    row = lax.broadcasted_iota(jnp.int32, (n, n), 0)
    col = lax.broadcasted_iota(jnp.int32, (n, n), 1)
    want = (col % 2) * (4 * size) + (col // 2 % 4) * size + col // 8
    return jnp.where(row == want, 1.0, 0.0).astype(jnp.bfloat16)


def dense_order(size):
    n = 16 * size
    row = lax.broadcasted_iota(jnp.int32, (n, n), 0)
    col = lax.broadcasted_iota(jnp.int32, (n, n), 1)
    want = (col % 4) * (4 * size) + (col // 4 % 4) * size + col // 16
    return jnp.where(row == want, 1.0, 0.0).astype(jnp.bfloat16)


def expand_body(values_ref, words_ref, dense_ref):
    for start, size in word_pieces(words_ref.shape[0]):
        lead, trail = kept_places(words_ref[start : start + size, :])
        both = mm(value_order(size), values_ref[8 * start : 8 * (start + size), :], (1, 0))
        half = 4 * size
        lead_vals, trail_vals = both[:half], both[half:]
        placed = jnp.concatenate(
            [
                jnp.where(lead == p, lead_vals, jnp.where(trail == p, trail_vals, 0.0))
                for p in (0.0, 1.0, 2.0, 3.0)
            ],
            axis=0,
        ).astype(jnp.bfloat16)
        dense_ref[16 * start : 16 * (start + size), :] = mm(dense_order(size), placed, (0, 0)).astype(
            jnp.bfloat16
        )


def expand(values, words, row_blocks, col_blocks):
    rows, cols = words.shape[0] // row_blocks, words.shape[1] // col_blocks
    at = lambda i: (i if row_blocks > 1 else 0, i if col_blocks > 1 else 0)
    return call(
        expand_body,
        grid=(row_blocks * col_blocks,),
        in_specs=[pl.BlockSpec((8 * rows, cols), at), pl.BlockSpec((rows, cols), at)],
        out_specs=pl.BlockSpec((16 * rows, cols), at),
        out_shape=jax.ShapeDtypeStruct((16 * words.shape[0], words.shape[1]), jnp.bfloat16),
        cost_estimate=pl.CostEstimate(flops=10**9 * 4, bytes_accessed=3 * 10**7, transcendentals=0),
    )(values, words)


def compress_into(dense, words_ref, out_ref):
    for start, size in word_pieces(words_ref.shape[0]):
        lead, trail = kept_places(words_ref[start : start + size, :])
        ordered = mm(dense_order(size), dense[16 * start : 16 * (start + size)], (1, 0))
        half = 4 * size
        lead_vals = jnp.zeros(lead.shape, jnp.float32)
        trail_vals = lead_vals
        for p in range(4):
            part = ordered[p * half : (p + 1) * half]
            lead_vals = jnp.where(lead == float(p), part, lead_vals)
            trail_vals = jnp.where(trail == float(p), part, trail_vals)
        both = jnp.concatenate([lead_vals, trail_vals], axis=0).astype(jnp.bfloat16)
        out_ref[8 * start : 8 * (start + size), :] = mm(value_order(size), both, (0, 0)).astype(
            jnp.bfloat16
        )


def swiglu_body(last, hidden_first, row_ref, cot_ref, gate_ref, up_ref, down_ref, *rest):
    hidden_ref, gate_grad_ref, up_grad_ref, gate_acc, up_acc, hid_acc = rest
    step = pl.program_id(0)

    @pl.when(step == 0)
    def _():
        gate_acc[...] = jnp.zeros_like(gate_acc)
        up_acc[...] = jnp.zeros_like(up_acc)
        hid_acc[...] = jnp.zeros_like(hid_acc)

    gate_acc[...] += mm(row_ref[0], gate_ref[...], (1, 0))
    up_acc[...] += mm(row_ref[0], up_ref[...], (1, 0))
    hid_acc[...] += mm(cot_ref[0], down_ref[...], (1, 1 if hidden_first else 0))

    @pl.when(step == last)
    def _():
        gate_pre, up_pre, hid_grad = gate_acc[...], up_acc[...], hid_acc[...]
        sig = jax.nn.sigmoid(gate_pre)
        active = gate_pre * sig
        hidden_ref[...] = (active * up_pre).astype(jnp.bfloat16)
        gate_grad_ref[...] = (hid_grad * up_pre * sig * (1.0 + gate_pre * (1.0 - sig))).astype(
            jnp.bfloat16
        )
        up_grad_ref[...] = (hid_grad * active).astype(jnp.bfloat16)


def swiglu_steps(both, w_gate, w_up, w_down, hidden_first):
    parts, rows, width = both.shape
    width //= 2
    hid = w_gate.shape[1]
    weight = pl.BlockSpec((width, hid), lambda i: (i, 0))
    down = pl.BlockSpec((hid, width), lambda i: (0, i)) if hidden_first else weight
    return call(
        functools.partial(swiglu_body, parts - 1, hidden_first),
        grid=(parts,),
        in_specs=[
            pl.BlockSpec((1, rows, width), lambda i: (i, 0, 0)),
            pl.BlockSpec((1, rows, width), lambda i: (i, 0, 1)),
            weight,
            weight,
            down,
        ],
        out_specs=[pl.BlockSpec((rows, hid), lambda i: (0, 0))] * 3,
        out_shape=[jax.ShapeDtypeStruct((rows, hid), jnp.bfloat16)] * 3,
        scratch_shapes=[pltpu.VMEM((rows, hid), jnp.float32)] * 3,
        cost_estimate=pl.CostEstimate(
            flops=6 * rows * hid * width * parts, bytes_accessed=2 * 10**7, transcendentals=rows * hid
        ),
    )(both, both, w_gate, w_up, w_down)


def back_body(gate_grad_ref, up_grad_ref, gate_ref, up_ref, out_ref):
    out_ref[0] = (
        mm(gate_grad_ref[...], gate_ref[...], (1, 1)) + mm(up_grad_ref[...], up_ref[...], (1, 1))
    ).astype(out_ref.dtype)


def back(gate_grad, up_grad, w_gate, w_up, parts):
    rows, hid = gate_grad.shape
    width = w_gate.shape[0] // parts
    whole = pl.BlockSpec((rows, hid), lambda i: (0, 0))
    weight = pl.BlockSpec((width, hid), lambda i: (i, 0))
    return call(
        back_body,
        grid=(parts,),
        in_specs=[whole, whole, weight, weight],
        out_specs=pl.BlockSpec((1, rows, width), lambda i: (i, 0, 0)),
        out_shape=jax.ShapeDtypeStruct((parts, rows, width), jnp.bfloat16),
        cost_estimate=pl.CostEstimate(
            flops=4 * rows * hid * width * parts, bytes_accessed=2 * 10**7, transcendentals=0
        ),
    )(gate_grad, up_grad, w_gate, w_up)


def gate_up_body(row_ref, gate_grad_ref, up_grad_ref, gate_words, up_words, gate_out, up_out):
    rows = row_ref[0]
    compress_into(mm(rows, gate_grad_ref[...], (0, 0)).astype(jnp.bfloat16), gate_words, gate_out)
    compress_into(mm(rows, up_grad_ref[...], (0, 0)).astype(jnp.bfloat16), up_words, up_out)


def gate_up_values(both, gate_grad, up_grad, gate_words, up_words):
    parts, rows, width = both.shape
    width //= 2
    hid = gate_grad.shape[1]
    grads = pl.BlockSpec((rows, hid), lambda i: (0, 0))
    words = pl.BlockSpec((width // 16, hid), lambda i: (i, 0))
    return call(
        gate_up_body,
        grid=(parts,),
        in_specs=[pl.BlockSpec((1, rows, width), lambda i: (i, 0, 0)), grads, grads, words, words],
        out_specs=[pl.BlockSpec((width // 2, hid), lambda i: (i, 0))] * 2,
        out_shape=[jax.ShapeDtypeStruct((parts * width // 2, hid), jnp.bfloat16)] * 2,
        cost_estimate=pl.CostEstimate(
            flops=8 * rows * hid * width * parts, bytes_accessed=2 * 10**7, transcendentals=0
        ),
    )(both, gate_grad, up_grad, gate_words, up_words)


def down_body(hidden_ref, cot_ref, words_ref, out_ref):
    compress_into(mm(hidden_ref[...], cot_ref[0], (0, 0)).astype(jnp.bfloat16), words_ref, out_ref)


def down_values_of(both, hidden, words):
    parts, rows, width = both.shape
    width //= 2
    hid = hidden.shape[1]
    return call(
        down_body,
        grid=(parts,),
        in_specs=[
            pl.BlockSpec((rows, hid), lambda i: (0, 0)),
            pl.BlockSpec((1, rows, width), lambda i: (i, 0, 1)),
            pl.BlockSpec((hid // 16, width), lambda i: (0, i)),
        ],
        out_specs=pl.BlockSpec((hid // 2, width), lambda i: (0, i)),
        out_shape=jax.ShapeDtypeStruct((hid // 2, parts * width), jnp.bfloat16),
        cost_estimate=pl.CostEstimate(
            flops=4 * rows * hid * width * parts, bytes_accessed=2 * 10**7, transcendentals=0
        ),
    )(hidden, both, words)


def weight_body(row_ref, cot_ref, steps_ref, *outs):
    hid = steps_ref.shape[1] // 3
    rows, cots = row_ref[0], cot_ref[0]
    outs[0][...] = mm(rows, steps_ref[:, :hid], (0, 0)).astype(jnp.bfloat16)
    outs[1][...] = mm(rows, steps_ref[:, hid : 2 * hid], (0, 0)).astype(jnp.bfloat16)
    outs[2][...] = mm(cots, steps_ref[:, 2 * hid :], (0, 0)).astype(jnp.bfloat16)


def weight_grads(both, steps):
    parts, rows, width = both.shape
    width //= 2
    hid = steps.shape[1] // 3
    cuts = 7 if width % 896 == 0 and parts == 1 else 1
    piece = width // cuts
    return call(
        weight_body,
        grid=(parts, cuts),
        in_specs=[
            pl.BlockSpec((1, rows, piece), lambda i, j: (i, 0, j)),
            pl.BlockSpec((1, rows, piece), lambda i, j: (i, 0, cuts + j)),
            pl.BlockSpec((rows, 3 * hid), lambda i, j: (0, 0)),
        ],
        out_specs=[pl.BlockSpec((piece, hid), lambda i, j: (i * cuts + j, 0))] * 3,
        out_shape=[jax.ShapeDtypeStruct((parts * width, hid), jnp.bfloat16)] * 3,
        cost_estimate=pl.CostEstimate(
            flops=6 * rows * hid * width * parts, bytes_accessed=2 * 10**7, transcendentals=0
        ),
    )(both, both, steps)


def slot_masks(route_block, weight_block, own, experts, capacity):
    flat = (route_block.reshape(-1) - own + experts) % experts
    count = flat.shape[0]
    place = jnp.arange(count, dtype=jnp.int32)
    same = (flat[:, None] == flat[None, :]) & (place[None, :] < place[:, None])
    slot_index = flat * capacity + jnp.sum(same, axis=1, dtype=jnp.int32)
    slots = jnp.arange(experts * capacity, dtype=jnp.int32)
    first, second = slot_index.reshape(-1, 2)[:, 0], slot_index.reshape(-1, 2)[:, 1]
    hit_first = slots[:, None] == first[None, :]
    hit_second = slots[:, None] == second[None, :]
    taken = (hit_first | hit_second).astype(jnp.bfloat16)
    scales = jnp.sum(
        jnp.where(hit_first, weight_block[None, :, 0], 0.0)
        + jnp.where(hit_second, weight_block[None, :, 1], 0.0),
        axis=1,
    )
    return taken, scales


def swapped(block, axis, distance):
    count = lax.axis_size(axis)
    return lax.ppermute(block, axis, [(i, i ^ distance) for i in range(count)])


def shifted(block, axis, distance):
    count = lax.axis_size(axis)
    return lax.ppermute(block, axis, [(i, (i + distance) % count) for i in range(count)])


def gather_parts(block, beside):
    if lax.axis_size("tensor") != 4:
        return lax.all_gather(block, "tensor", axis=0), beside
    place = lax.axis_index("tensor")
    low_chip, low_core = place // 2 == 0, place % 2 == 0
    far, beside = lax.optimization_barrier((swapped(block, "tensor", 2), beside))
    mine = jnp.stack([jnp.where(low_chip, block, far), jnp.where(low_chip, far, block)])
    near = swapped(mine, "tensor", 1)
    both = jnp.stack([jnp.where(low_core, mine, near), jnp.where(low_core, near, mine)], axis=1)
    return both.reshape((4,) + block.shape), beside


def gather_groups(block):
    count, rows = lax.axis_size("expert"), block.shape[0]
    arrived = [shifted(block, "expert", k) for k in range(count - 1, 0, -1)] + [block]
    start = (count - 1 - lax.axis_index("expert")) * rows
    return lax.dynamic_slice_in_dim(jnp.concatenate(arrived + arrived, axis=0), start, count * rows, 0)


def added(a, b):
    return a.astype(jnp.float32) + b.astype(jnp.float32)


def scatter_parts(parts, later=()):
    if lax.axis_size("tensor") != 4:
        total = lax.psum_scatter(parts, "tensor", scatter_dimension=0, tiled=True)[0]
        return total.astype(jnp.float32), later
    place = lax.axis_index("tensor")
    chip, core = place // 2, place % 2
    split = parts.reshape((2, 2) + parts.shape[1:])
    send = lax.dynamic_index_in_dim(split, 1 - core, 1, keepdims=False)
    keep = lax.dynamic_index_in_dim(split, core, 1, keepdims=False)
    near, later = lax.optimization_barrier((swapped(send, "tensor", 1), later))
    summed = added(keep, near).astype(jnp.bfloat16)
    send = lax.dynamic_index_in_dim(summed, 1 - chip, 0, keepdims=False)
    keep = lax.dynamic_index_in_dim(summed, chip, 0, keepdims=False)
    return added(keep, swapped(send, "tensor", 2)), later


def scatter_batches(block, axis):
    if lax.axis_size("dp") != 2:
        return lax.psum_scatter(block, "dp", scatter_dimension=axis, tiled=True).astype(jnp.float32)
    own = lax.axis_index("dp")
    size = block.shape[axis] // 2
    send = lax.dynamic_slice_in_dim(block, (1 - own) * size, size, axis)
    keep = lax.dynamic_slice_in_dim(block, own * size, size, axis)
    return added(keep, swapped(send, "dp", 1))


def shards(
    tokens,
    cotangent,
    routes,
    route_weights,
    gate_values,
    up_values,
    down_values,
    gate_words,
    up_words,
    down_words,
    res_gate,
    res_up,
    res_down,
):
    experts = lax.axis_size("expert")
    dp_count = lax.axis_size("dp")
    parts = lax.axis_size("tensor")
    tok_count, width = tokens.shape
    capacity = 5 * tok_count // (2 * experts)
    local = jnp.concatenate([tokens, cotangent], axis=1)
    taken, scales = slot_masks(routes, route_weights, lax.axis_index("expert"), experts, capacity)
    slot_local = mm(taken, local, (1, 0))
    slot_local = jnp.concatenate(
        [slot_local[:, :width], slot_local[:, width:] * scales[:, None]], axis=1
    ).astype(jnp.bfloat16)
    blocks = [slot_local[k * capacity : (k + 1) * capacity] for k in range(experts)]
    arrived = [blocks[0]] + [shifted(blocks[k], "expert", k) for k in range(1, experts)]
    slots = jnp.concatenate(arrived, axis=0)

    pair_both = lax.all_gather(local, ("tensor", "dp"), axis=0).reshape(
        parts, dp_count * tok_count, 2 * width
    )

    gate_dense = expand(gate_values[0], gate_words[0], parts, 1)
    up_dense = expand(up_values[0], up_words[0], parts, 1)
    down_dense = expand(down_values[0], down_words[0], 1, parts)

    res_hidden, res_gate_step, res_up_step = swiglu_steps(pair_both, res_gate, res_up, res_down, False)
    res_back = back(res_gate_step, res_up_step, res_gate, res_up, parts)

    slot_both, (gate_dense, up_dense, down_dense) = gather_parts(slots, (gate_dense, up_dense, down_dense))
    slot_both, res_hidden, res_gate_step, res_up_step, res_back = lax.optimization_barrier(
        (slot_both, res_hidden, res_gate_step, res_up_step, res_back)
    )
    hidden, gate_grad, up_grad = swiglu_steps(slot_both, gate_dense, up_dense, down_dense, True)
    slot_back = back(gate_grad, up_grad, gate_dense, up_dense, parts)
    slot_back, hidden = lax.optimization_barrier((slot_back, hidden))
    down_terms = down_values_of(slot_both, hidden, down_words[0])
    slot_share, (down_terms, gate_grad, up_grad) = scatter_parts(slot_back, (down_terms, gate_grad, up_grad))
    gate_terms, up_terms = gate_up_values(slot_both, gate_grad, up_grad, gate_words[0], up_words[0])
    slot_share = slot_share.astype(jnp.bfloat16)
    blocks = [slot_share[k * capacity : (k + 1) * capacity] for k in range(experts)]
    returned = [blocks[0]] + [shifted(blocks[k], "expert", -k) for k in range(1, experts)]
    res_share = scatter_batches(scatter_parts(res_back)[0].astype(jnp.bfloat16), 0)
    combined = res_share + mm(taken, jnp.concatenate(returned, axis=0), (0, 0))

    gate_share = scatter_batches(gate_terms, 0)
    up_share = scatter_batches(up_terms, 0)
    down_share = scatter_batches(down_terms, 1)

    if parts == experts:
        turned = lax.ppermute(
            local,
            ("expert", "tensor"),
            [(e * parts + t, t * parts + e) for e in range(experts) for t in range(parts)],
        )
        all_rows = lax.all_gather(turned, ("tensor", "dp"), axis=0).reshape(1, -1, 2 * width)
        steps = jnp.concatenate([res_gate_step, res_up_step, res_hidden], axis=1)
        steps = gather_groups(steps)
        res_sums = weight_grads(all_rows, steps)
    else:
        steps = jnp.concatenate([res_gate_step, res_up_step, res_hidden], axis=1)
        res_sums = [
            lax.psum_scatter(term, "expert", scatter_dimension=0, tiled=True)
            for term in weight_grads(pair_both, steps)
        ]
    return (
        combined.astype(jnp.bfloat16),
        gate_share.astype(jnp.bfloat16)[None],
        up_share.astype(jnp.bfloat16)[None],
        down_share.astype(jnp.bfloat16)[None],
        res_sums[0],
        res_sums[1],
        res_sums[2],
    )


def solution(mesh):
    in_specs = (
        P(("dp", "expert"), "tensor"),
        P(("dp", "expert"), "tensor"),
        P(("dp", "expert"), None),
        P(("dp", "expert"), None),
        P("expert", None, "tensor"),
        P("expert", None, "tensor"),
        P("expert", "tensor", None),
        P("expert", None, "tensor"),
        P("expert", None, "tensor"),
        P("expert", "tensor", None),
        P(None, ("dp", "tensor")),
        P(None, ("dp", "tensor")),
        P(None, ("dp", "tensor")),
    )
    out_specs = (
        P(("dp", "expert"), "tensor"),
        P("expert", "dp", "tensor"),
        P("expert", "dp", "tensor"),
        P("expert", "tensor", "dp"),
        P("expert", ("dp", "tensor")),
        P("expert", ("dp", "tensor")),
        P("expert", ("dp", "tensor")),
    )
    return jax.shard_map(shards, mesh=mesh, in_specs=in_specs, out_specs=out_specs, check_vma=False)
```
